32 devices in a mesh: lst: 4 (over y, x), night: 8 (over z, core).
Axes of the slice: x: 2, y: 2, z: 4, core: 2. Of those that a mesh axis runs over, the one named last changes fastest.
Arguments:
- visibility: bfloat16 [8, 32, 16, 2, 1536], P('night', 'lst'), may hold values from -18 to 18
- flags: int32 [8, 32, 16, 1536], P('night', 'lst'), may hold values 0 or 1
- counts: int32 [8, 32], P('night', 'lst'), may hold values from 1 to 4
- offsets: int32 [8], P('night'), may hold values from -6 to 6, as said below
- fraction: float32 [8], P('night'), may hold values from 0 to 1
- gains: float32 [8, 2, 1536], P('night'), may hold values from -6 to 6
- inverse_var: float32 [8, 1536], P('night'), may hold values from 0.005 to 0.05
- prior: float32 [1536], replicated, may hold values from 0.5 to 5
Outputs:
- binned: bfloat16 [32, 16, 2, 1536], P('lst')
- weight_total: float32 [32, 16, 1536], P('lst')
The draws below stay inside these ranges and needn't reach their ends.
Inputs may be any that keep to these rules, and one draw needn't show every extreme that they name: `offsets`: both -6 and 6 occur among the nights.
All inputs are finite; a program needn't handle non-finite values. No bound on the sum of `flags` on one device may be relied on, other than what follows from the above.
Results may differ from the reference program's by a relative error of at most 0.009.
Values may be sent and summed in bfloat16 or wider, within the bound.
A program may use at most 64 MiB of HBM per device.

```python
import math
import jax
import jax.numpy as jnp
from jax import lax

F = 1536
B = 16
L = 32
NIGHTS = 8
MAXOFF = 6


def draw_offsets(key, part):
    first_key, second_key = jax.random.split(key, 2)
    values = jax.random.randint(first_key, (NIGHTS,), -MAXOFF, MAXOFF + 1)
    order = jax.random.permutation(second_key, NIGHTS)
    values = values.at[order[0]].set(MAXOFF)
    values = values.at[order[1]].set(-MAXOFF)
    return values.astype(jnp.int32)


def touch_ends(values, rng, least, top_value):
    longest = values.shape.index(max(values.shape))
    spots = []
    for shift in (0, 1):
        where = [jax.random.randint(jax.random.fold_in(rng, axis), (), 0, length) for axis, length in enumerate(values.shape)]
        where[longest] = (where[longest] + shift) % values.shape[longest]
        spots.append(tuple(where))
    return values.at[spots[0]].set(least).at[spots[1]].set(top_value)


def block_levels(stream_key, dims, shards, smallest, top_value):
    def one(dim, blocks):
        draws = jax.random.uniform(jax.random.fold_in(jax.random.fold_in(stream_key, 6), dim), (blocks,), jnp.float32, smallest / len(shards), top_value / len(shards))
        return jnp.repeat(jnp.exp(draws), dims[dim] // blocks).reshape((-1,) + (1,) * (len(dims) - dim - 1))

    factor_of = one(*shards[0])
    for cut in shards[1:]:
        factor_of = factor_of * one(*cut)
    return factor_of


def centred(stream_key, shape, deviation, bound, cuts=(), dtype=jnp.bfloat16):
    result = deviation * jax.random.normal(stream_key, shape, jnp.float32)
    if cuts:
        result = result * block_levels(stream_key, shape, cuts, -0.22, 0.18)
    return jnp.clip(result, -bound, bound).astype(dtype)


def setup_inputs(seed: int = 0) -> dict:
    splits = jax.random.split(jax.random.key(seed), 9)
    return {
        "visibility": centred(splits[0], (NIGHTS, L, B, 2, F), 3.0, 18.0, ((0, 8), (1, 4))),
        "flags": touch_ends((jax.random.randint(splits[1], (NIGHTS, L, B, F), 0, 8) < 7).astype(jnp.int32), jax.random.fold_in(splits[1], 1), 0, 1),
        "counts": touch_ends(jax.random.randint(splits[2], (NIGHTS, L), 1, 5), jax.random.fold_in(splits[2], 1), 1, 4).astype(jnp.int32),
        "offsets": draw_offsets(jax.random.fold_in(splits[8], 71), 0),
        "fraction": jnp.clip(1.0 * jax.random.uniform(splits[4], (NIGHTS,), jnp.float32) ** block_levels(splits[4], (NIGHTS,), ((0, 8),), -0.2, 0.2), 0.0, 1.0),
        "gains": centred(splits[5], (NIGHTS, 2, F), 1.0, 6.0, ((0, 8),), jnp.float32),
        "inverse_var": jnp.clip(jnp.exp(math.log(0.05) - 2.3025851 * jax.random.uniform(splits[6], (NIGHTS, F), jnp.float32) ** block_levels(splits[6], (NIGHTS, F), ((0, 8),), -0.2, 0.2)), 0.005, 0.05),
        "prior": jnp.clip(jnp.exp(jax.random.uniform(splits[7], (F,), jnp.float32, math.log(0.5), math.log(5.0))), 0.5, 5.0),
    }


def spline_taps(fraction):
    cube = fraction * fraction * fraction
    square = fraction * fraction
    first = (1.0 - fraction) ** 3 / 6.0
    second = (3.0 * cube - 6.0 * square + 4.0) / 6.0
    third = (-3.0 * cube + 3.0 * square + 3.0 * fraction + 1.0) / 6.0
    fourth = cube / 6.0
    return jnp.stack([first, second, third, fourth], axis=-1)


def reference(visibility, flags, counts, offsets, fraction, gains, inverse_var, prior):
    def one_night(carry, inputs):
        num_sum, denominator_sum = carry
        vis_night, flag_night, night_sample_count, gain_night, inv_night, shift_night, frac_night = inputs
        scale = (flag_night * night_sample_count[:, None, None]).astype(jnp.float32) * inv_night[None, None, :]
        weight = scale.astype(jnp.bfloat16)
        real_part = vis_night[:, :, 0].astype(jnp.float32)
        imag_part = vis_night[:, :, 1].astype(jnp.float32)
        gain_re = gain_night[0][None, None, :]
        gain_im = gain_night[1][None, None, :]
        cal_re = gain_re * real_part - gain_im * imag_part
        cal_im = gain_re * imag_part + gain_im * real_part
        weighted = (scale[:, :, None, :] * jnp.stack([cal_re, cal_im], axis=2)).astype(jnp.bfloat16)
        taps = lax.optimization_barrier(spline_taps(frac_night).astype(jnp.bfloat16)).astype(jnp.float32)
        weighted_f = weighted.astype(jnp.float32)
        weight_f = weight.astype(jnp.float32)
        for tap_idx in range(4):
            amount = (shift_night - tap_idx + 1).astype(jnp.int32)
            num_sum = num_sum + taps[tap_idx] * jnp.roll(weighted_f, amount, axis=0)
            denominator_sum = denominator_sum + taps[tap_idx] * jnp.roll(weight_f, amount, axis=0)
        return (num_sum, denominator_sum), None

    num_zero = jnp.zeros(visibility.shape[1:], jnp.float32)
    den_zero = jnp.zeros(flags.shape[1:], jnp.float32)
    (num_sum, denominator_sum), unused = lax.scan(one_night, (num_zero, den_zero),
                                          (visibility, flags, counts, gains, inverse_var, offsets, fraction))
    binned = (num_sum / (denominator_sum[:, :, None, :] + prior[None, None, None, :])).astype(jnp.bfloat16)
    return binned, denominator_sum
```

```python
import functools
import math

import jax
import jax.numpy as jnp
from jax import lax
from jax.experimental import pallas as pl
from jax.experimental.pallas import tpu as pltpu
from jax.sharding import PartitionSpec as P

LANES = 128
REACH = 7
SHIFTS = 16


def spline_taps(fraction):
    cube = fraction * fraction * fraction
    square = fraction * fraction
    first = (1.0 - fraction) ** 3 / 6.0
    second = (3.0 * cube - 6.0 * square + 4.0) / 6.0
    third = (-3.0 * cube + 3.0 * square + 3.0 * fraction + 1.0) / 6.0
    fourth = cube / 6.0
    return jnp.stack([first, second, third, fourth], axis=-1)


def kernel(
    lsts, chips, rows, blocks,
    coef_ref, slab_ref, prior_ref, out_ref,
    ext, pair_out, pair_in, own, sum_out, sum_in,
    near_s, near_r, far_s, far_r, pair_s, pair_r, sum_s, sum_r, gat_s, gat_r, fwd_s, fwd_r,
):
    lst = lax.axis_index("lst")
    night = lax.axis_index("night")
    chip = night // 2
    core = night % 2
    partner = night + 1 - 2 * core
    groups = math.gcd(blocks, chips)
    splits = chips // groups
    phases = blocks // groups
    part = rows // splits
    piece = part // 2
    two_hops = lsts == 4
    if two_hops:
        odd = lst % 2
        near_to, near_at = lst + 1 - 2 * odd, 2 * odd * rows
        far_to, far_at = (lst + 2) % 4, 2 * odd * rows
        far_from = (2 - 2 * odd) * rows
    else:
        near_to, near_at = (lst + 1) % lsts, 0
        far_to, far_at = (lst + lsts - 1) % lsts, 2 * rows
        far_from = rows

    def remote(src, dst, send, recv, l, n):
        return pltpu.make_async_remote_copy(
            src_ref=src, dst_ref=dst, send_sem=send, recv_sem=recv,
            device_id={"lst": l, "night": n}, device_id_type=pl.DeviceIdType.MESH)

    others = [((chip + d) % chips) * 2 + core for d in range(1, chips)]
    barrier = pltpu.get_barrier_semaphore()
    greeted = [(near_to, night), (far_to, night), (lst, partner)] + [(lst, n) for n in others]
    for l, n in greeted:
        pl.semaphore_signal(barrier, inc=1, device_id={"lst": l, "night": n}, device_id_type=pl.DeviceIdType.MESH)
    pl.semaphore_wait(barrier, len(greeted))

    def lanes(block):
        return pl.ds(pl.multiple_of(block * LANES, LANES), LANES)

    def near(t):
        return remote(ext.at[t, pl.ds(rows, rows)], ext.at[t, pl.ds(near_at, rows)],
                      near_s.at[t], near_r.at[t], near_to, night)

    def far(t):
        return remote(ext.at[t, pl.ds(far_from, rows)], ext.at[t, pl.ds(far_at, rows)],
                      far_s.at[t], far_r.at[t], far_to, night)

    def pass_on(t):
        near(t).wait_recv()
        if two_hops:
            far(t).start()

    def pair(s):
        return remote(pair_out.at[s], pair_in.at[s], pair_s.at[s], pair_r.at[s], lst, partner)

    def target(s):
        g, r = (s % chips) // splits, s % splits
        return (chip + 1 + g) % groups + ((chip // groups + 1 + r) % splits) * groups

    def toward(s):
        return remote(sum_out.at[s], sum_in.at[s], sum_s.at[s], sum_r.at[s], lst, target(s) * 2 + core)

    def place(owner, p, of_core):
        block = (owner % groups) * phases + p
        row = (owner // groups) * part + of_core * piece
        return out_ref.at[pl.ds(row, piece), :, :, lanes(block)]

    def gather(p, d):
        here = place(chip, p, core)
        i = p * chips + d
        return remote(here, here, gat_s.at[i], gat_r.at[i], lst, others[d - 1])

    def forward(p, d):
        here = place((chip + chips - d) % chips, p, core)
        i = p * chips + d
        return remote(here, here, fwd_s.at[i], fwd_r.at[i], lst, partner)

    def regrid(s, base, dst, index):
        t = s // splits

        def component(c, carry):
            acc = jnp.zeros((piece,) + ext.shape[3:], jnp.float32)
            for d in range(SHIFTS):
                window = ext[t, pl.ds(rows - REACH + d + base, piece), c]
                acc = acc + coef_ref[0, d] * window.astype(jnp.float32)
            dst[index, :, c] = acc.astype(dst.dtype)
            return carry

        lax.fori_loop(0, 3, component, 0)

    def first_part(s):
        base = ((chip // groups + 1 + s % splits) % splits) * part
        regrid(s, base + (1 - core) * piece, pair_out, s)
        pair(s).start()
        regrid(s, base + core * piece, own, s)

    def pair_sum(s):
        pair(s).wait_recv()
        both = own[s] + pair_in[s].astype(jnp.float32)
        if s % chips < chips - 1:
            sum_out[s] = both.astype(jnp.bfloat16)
            toward(s).start()
        else:
            own[s] = both

    def finish(p):
        total = own[p * chips + chips - 1]
        for k in range(chips - 1):
            toward(p * chips + k).wait_recv()
            total = total + sum_in[p * chips + k].astype(jnp.float32)
        block = (chip % groups) * phases + p
        prior = prior_ref[:, lanes(block)]
        den = total[:, 2]
        inverse = (den + prior[None])[:, None]
        row = (chip // groups) * part + core * piece
        out_ref[pl.ds(row, piece), 0:2, :, lanes(block)] = (total[:, 0:2] / inverse).astype(jnp.bfloat16)
        out_ref[pl.ds(row, piece), 2:3, :, lanes(block)] = den[:, None].astype(jnp.bfloat16)
        for d in range(1, chips):
            gather(p, d).start()
        forward(p, 0).start()

    def share(p):
        for d in range(1, chips):
            gather(p, d).wait_recv()
            forward(p, d).start()

    for t in range(blocks):
        block = ((chip + 1 + t % groups) % groups) * phases + t // groups
        ext[t, rows:2 * rows] = slab_ref[:, :, :, lanes(block)]
        near(t).start()
        if not two_hops:
            far(t).start()

    steps = phases * chips
    pass_on(0)
    for s in range(steps):
        t, p, k = s // splits, s // chips, s % chips
        if s % splits == 0:
            if t + 1 < blocks:
                pass_on(t + 1)
            far(t).wait_recv()
        first_part(s)
        if s > 0:
            pair_sum(s - 1)
        if p > 0 and k == min(1, chips - 1):
            finish(p - 1)
        if p > 0 and k == chips - 1:
            share(p - 1)
    pair_sum(steps - 1)
    finish(phases - 1)
    share(phases - 1)
    for p in range(phases):
        for d in range(chips):
            forward(p, d).wait()
            if d > 0:
                gather(p, d).wait_send()
    for s in range(steps):
        pair(s).wait_send()
        if s % chips < chips - 1:
            toward(s).wait_send()
    for t in range(blocks):
        near(t).wait_send()
        far(t).wait_send()


def shards(mesh, visibility, flags, counts, offsets, fraction, gains, inverse_var, prior):
    lsts, chips = mesh.shape["lst"], mesh.shape["night"] // 2
    rows, baselines, channels = visibility.shape[1], visibility.shape[2], visibility.shape[4]
    blocks = channels // LANES
    scale = (flags[0] * counts[0][:, None, None]).astype(jnp.float32) * inverse_var[0][None, None, :]
    weight = scale.astype(jnp.bfloat16)
    real_part = visibility[0, :, :, 0].astype(jnp.float32)
    imag_part = visibility[0, :, :, 1].astype(jnp.float32)
    gain_re, gain_im = gains[0, 0], gains[0, 1]
    cal_re = gain_re * real_part - gain_im * imag_part
    cal_im = gain_re * imag_part + gain_im * real_part
    slab = jnp.stack([(scale * cal_re).astype(jnp.bfloat16), (scale * cal_im).astype(jnp.bfloat16), weight], axis=1)
    taps = spline_taps(fraction)[0].astype(jnp.bfloat16).astype(jnp.float32)
    shift = jnp.arange(SHIFTS).reshape(SHIFTS, 1)
    wanted = jnp.arange(4).reshape(1, 4) - offsets[0] - 1 + REACH
    coef = jnp.sum(jnp.where(shift == wanted, taps[None, :], 0.0), axis=1).reshape(1, SHIFTS)

    groups = math.gcd(blocks, chips)
    splits = chips // groups
    phases = blocks // groups
    steps = phases * chips
    piece = rows // splits // 2
    tile = (piece, 3, baselines, LANES)
    dma = pltpu.SemaphoreType.DMA
    out = pl.pallas_call(
        functools.partial(kernel, lsts, chips, rows, blocks),
        out_shape=jax.ShapeDtypeStruct((rows, 3, baselines, channels), jnp.bfloat16),
        in_specs=[
            pl.BlockSpec(memory_space=pltpu.SMEM),
            pl.BlockSpec(memory_space=pltpu.VMEM),
            pl.BlockSpec(memory_space=pltpu.VMEM),
        ],
        out_specs=pl.BlockSpec(memory_space=pltpu.VMEM),
        scratch_shapes=[
            pltpu.VMEM((blocks, 3 * rows, 3, baselines, LANES), jnp.bfloat16),
            pltpu.VMEM((steps,) + tile, jnp.bfloat16),
            pltpu.VMEM((steps,) + tile, jnp.bfloat16),
            pltpu.VMEM((steps,) + tile, jnp.float32),
            pltpu.VMEM((steps,) + tile, jnp.bfloat16),
            pltpu.VMEM((steps,) + tile, jnp.bfloat16),
            dma((blocks,)), dma((blocks,)), dma((blocks,)), dma((blocks,)),
            dma((steps,)), dma((steps,)), dma((steps,)), dma((steps,)),
            dma((steps,)), dma((steps,)), dma((steps,)), dma((steps,)),
        ],
        compiler_params=pltpu.CompilerParams(
            collective_id=0, has_side_effects=True, vmem_limit_bytes=40 * 2**20),
    )(coef, slab, prior.reshape(1, channels))
    binned = jnp.swapaxes(out[:, 0:2], 1, 2)
    return binned, out[:, 2].astype(jnp.float32)


def solution(mesh):
    in_specs = (
        P("night", "lst", None, None, None),
        P("night", "lst", None, None),
        P("night", "lst"),
        P("night"),
        P("night"),
        P("night", None, None),
        P("night", None),
        P(),
    )
    out_specs = (P("lst", None, None, None), P("lst", None, None))
    return jax.shard_map(functools.partial(shards, mesh), mesh=mesh, in_specs=in_specs, out_specs=out_specs, check_vma=False)
```

```python
import functools
import math

import jax
import jax.numpy as jnp
from jax import lax
from jax.experimental import pallas as pl
from jax.experimental.pallas import tpu as pltpu
from jax.sharding import PartitionSpec as P

LANES = 128
REACH = 7
SHIFTS = 16


def spline_taps(fraction):
    cube = fraction * fraction * fraction
    square = fraction * fraction
    first = (1.0 - fraction) ** 3 / 6.0
    second = (3.0 * cube - 6.0 * square + 4.0) / 6.0
    third = (-3.0 * cube + 3.0 * square + 3.0 * fraction + 1.0) / 6.0
    fourth = cube / 6.0
    return jnp.stack([first, second, third, fourth], axis=-1)


def kernel(
    lsts, chips, rows, blocks,
    coef_ref, vis_ref, flags_ref, level_ref, gains_ref, prior_ref, out_ref,
    ext, pair_out, pair_in, own, sum_out, sum_in,
    near_s, near_r, far_s, far_r, pair_s, pair_r, sum_s, sum_r, gat_s, gat_r, fwd_s, fwd_r,
):
    lst = lax.axis_index("lst")
    night = lax.axis_index("night")
    chip = night // 2
    core = night % 2
    partner = night + 1 - 2 * core
    groups = math.gcd(blocks, chips)
    splits = chips // groups
    phases = blocks // groups
    part = rows // splits
    piece = part // 2
    two_hops = lsts == 4
    if two_hops:
        odd = lst % 2
        near_to, near_at = lst + 1 - 2 * odd, 2 * odd * rows
        far_to, far_at = (lst + 2) % 4, 2 * odd * rows
        far_from = (2 - 2 * odd) * rows
    else:
        near_to, near_at = (lst + 1) % lsts, 0
        far_to, far_at = (lst + lsts - 1) % lsts, 2 * rows
        far_from = rows

    def remote(src, dst, send, recv, l, n):
        return pltpu.make_async_remote_copy(
            src_ref=src, dst_ref=dst, send_sem=send, recv_sem=recv,
            device_id={"lst": l, "night": n}, device_id_type=pl.DeviceIdType.MESH)

    others = [((chip + d) % chips) * 2 + core for d in range(1, chips)]
    barrier = pltpu.get_barrier_semaphore()
    greeted = [(near_to, night), (far_to, night), (lst, partner)] + [(lst, n) for n in others]
    for l, n in greeted:
        pl.semaphore_signal(barrier, inc=1, device_id={"lst": l, "night": n}, device_id_type=pl.DeviceIdType.MESH)

    def lanes(block):
        return pl.ds(pl.multiple_of(block * LANES, LANES), LANES)

    def near(t):
        return remote(ext.at[t, pl.ds(rows, rows)], ext.at[t, pl.ds(near_at, rows)],
                      near_s.at[t], near_r.at[t], near_to, night)

    def far(t):
        return remote(ext.at[t, pl.ds(far_from, rows)], ext.at[t, pl.ds(far_at, rows)],
                      far_s.at[t], far_r.at[t], far_to, night)

    def pass_on(t):
        near(t).wait_recv()
        if two_hops:
            far(t).start()

    def pair(s):
        return remote(pair_out.at[s], pair_in.at[s], pair_s.at[s], pair_r.at[s], lst, partner)

    def target(s):
        g, r = (s % chips) // splits, s % splits
        return (chip + 1 + g) % groups + ((chip // groups + 1 + r) % splits) * groups

    def toward(s):
        return remote(sum_out.at[s], sum_in.at[s], sum_s.at[s], sum_r.at[s], lst, target(s) * 2 + core)

    def place(owner, p, of_core):
        block = (owner % groups) * phases + p
        row = (owner // groups) * part + of_core * piece
        return out_ref.at[pl.ds(row, piece), :, :, lanes(block)]

    def gather(p, d):
        here = place(chip, p, core)
        i = p * chips + d
        return remote(here, here, gat_s.at[i], gat_r.at[i], lst, others[d - 1])

    def forward(p, d):
        here = place((chip + chips - d) % chips, p, core)
        i = p * chips + d
        return remote(here, here, fwd_s.at[i], fwd_r.at[i], lst, partner)

    def regrid(s, base, dst, index):
        t = s // splits

        def component(c, carry):
            acc = jnp.zeros((piece,) + ext.shape[3:], jnp.float32)
            for d in range(SHIFTS):
                window = ext[t, pl.ds(rows - REACH + d + base, piece), c]
                acc = acc + coef_ref[0, d] * window.astype(jnp.float32)
            dst[index, :, c] = acc.astype(dst.dtype)
            return carry

        lax.fori_loop(0, 3, component, 0)

    def first_part(s):
        base = ((chip // groups + 1 + s % splits) % splits) * part
        regrid(s, base + (1 - core) * piece, pair_out, s)
        pair(s).start()
        regrid(s, base + core * piece, own, s)

    def pair_sum(s):
        pair(s).wait_recv()
        both = own[s] + pair_in[s].astype(jnp.float32)
        if s % chips < chips - 1:
            sum_out[s] = both.astype(jnp.bfloat16)
            toward(s).start()
        else:
            own[s] = both

    def finish(p):
        total = own[p * chips + chips - 1]
        for k in range(chips - 1):
            toward(p * chips + k).wait_recv()
            total = total + sum_in[p * chips + k].astype(jnp.float32)
        block = (chip % groups) * phases + p
        prior = prior_ref[:, lanes(block)]
        den = total[:, 2]
        inverse = (den + prior[None])[:, None]
        row = (chip // groups) * part + core * piece
        out_ref[pl.ds(row, piece), 0:2, :, lanes(block)] = (total[:, 0:2] / inverse).astype(jnp.bfloat16)
        out_ref[pl.ds(row, piece), 2:3, :, lanes(block)] = den[:, None].astype(jnp.bfloat16)
        for d in range(1, chips):
            gather(p, d).start()
        forward(p, 0).start()

    def share(p):
        for d in range(1, chips):
            gather(p, d).wait_recv()
            forward(p, d).start()

    for t in range(blocks):
        block = ((chip + 1 + t % groups) % groups) * phases + t // groups
        scale = flags_ref[:, :, lanes(block)].astype(jnp.float32) * level_ref[:, :, lanes(block)]
        real_part = vis_ref[:, 0, :, lanes(block)].astype(jnp.float32)
        imag_part = vis_ref[:, 1, :, lanes(block)].astype(jnp.float32)
        gain_re = gains_ref[0:1, lanes(block)][None]
        gain_im = gains_ref[1:2, lanes(block)][None]
        cal_re = gain_re * real_part - gain_im * imag_part
        cal_im = gain_re * imag_part + gain_im * real_part
        ext[t, rows:2 * rows, 0] = (scale * cal_re).astype(jnp.bfloat16)
        ext[t, rows:2 * rows, 1] = (scale * cal_im).astype(jnp.bfloat16)
        ext[t, rows:2 * rows, 2] = scale.astype(jnp.bfloat16)
    pl.semaphore_wait(barrier, len(greeted))

    for t in range(blocks):
        near(t).start()
        if not two_hops:
            far(t).start()

    steps = phases * chips
    for t in range(min(1, blocks)):
        pass_on(t)
    for s in range(steps):
        t, p, k = s // splits, s // chips, s % chips
        if s % splits == 0:
            if t + 1 < blocks:
                pass_on(t + 1)
        if s > 0:
            pair_sum(s - 1)
        if p > 0 and k == min(1, chips - 1):
            finish(p - 1)
        if p > 0 and k == chips - 1:
            share(p - 1)
        if s % splits == 0:
            far(t).wait_recv()
        first_part(s)
    pair_sum(steps - 1)
    finish(phases - 1)
    share(phases - 1)
    for p in range(phases):
        for d in range(chips):
            forward(p, d).wait()
            if d > 0:
                gather(p, d).wait_send()
    for s in range(steps):
        pair(s).wait_send()
        if s % chips < chips - 1:
            toward(s).wait_send()
    for t in range(blocks):
        near(t).wait_send()
        far(t).wait_send()


def shards(mesh, visibility, flags, counts, offsets, fraction, gains, inverse_var, prior):
    lsts, chips = mesh.shape["lst"], mesh.shape["night"] // 2
    rows, baselines, channels = visibility.shape[1], visibility.shape[2], visibility.shape[4]
    blocks = channels // LANES
    level = (counts[0].astype(jnp.float32)[:, None] * inverse_var[0][None, :])[:, None, :]
    taps = spline_taps(fraction)[0].astype(jnp.bfloat16).astype(jnp.float32)
    shift = jnp.arange(SHIFTS).reshape(SHIFTS, 1)
    wanted = jnp.arange(4).reshape(1, 4) - offsets[0] - 1 + REACH
    coef = jnp.sum(jnp.where(shift == wanted, taps[None, :], 0.0), axis=1).reshape(1, SHIFTS)

    groups = math.gcd(blocks, chips)
    splits = chips // groups
    phases = blocks // groups
    steps = phases * chips
    piece = rows // splits // 2
    tile = (piece, 3, baselines, LANES)
    dma = pltpu.SemaphoreType.DMA
    out = pl.pallas_call(
        functools.partial(kernel, lsts, chips, rows, blocks),
        out_shape=jax.ShapeDtypeStruct((rows, 3, baselines, channels), jnp.bfloat16),
        in_specs=[
            pl.BlockSpec(memory_space=pltpu.SMEM),
        ] + [pl.BlockSpec(memory_space=pltpu.VMEM)] * 5,
        out_specs=pl.BlockSpec(memory_space=pltpu.VMEM),
        scratch_shapes=[
            pltpu.VMEM((blocks, 3 * rows, 3, baselines, LANES), jnp.bfloat16),
            pltpu.VMEM((steps,) + tile, jnp.bfloat16),
            pltpu.VMEM((steps,) + tile, jnp.bfloat16),
            pltpu.VMEM((steps,) + tile, jnp.float32),
            pltpu.VMEM((steps,) + tile, jnp.bfloat16),
            pltpu.VMEM((steps,) + tile, jnp.bfloat16),
            dma((blocks,)), dma((blocks,)), dma((blocks,)), dma((blocks,)),
            dma((steps,)), dma((steps,)), dma((steps,)), dma((steps,)),
            dma((steps,)), dma((steps,)), dma((steps,)), dma((steps,)),
        ],
        compiler_params=pltpu.CompilerParams(
            collective_id=0, has_side_effects=True, vmem_limit_bytes=40 * 2**20),
    )(coef, jnp.swapaxes(visibility[0], 1, 2), flags[0], level, gains[0], prior.reshape(1, channels))
    binned = jnp.swapaxes(out[:, 0:2], 1, 2)
    return binned, out[:, 2].astype(jnp.float32)


def solution(mesh):
    in_specs = (
        P("night", "lst", None, None, None),
        P("night", "lst", None, None),
        P("night", "lst"),
        P("night"),
        P("night"),
        P("night", None, None),
        P("night", None),
        P(),
    )
    out_specs = (P("lst", None, None, None), P("lst", None, None))
    return jax.shard_map(functools.partial(shards, mesh), mesh=mesh, in_specs=in_specs, out_specs=out_specs, check_vma=False)
```

```python
import functools
import math

import jax
import jax.numpy as jnp
from jax import lax
from jax.experimental import pallas as pl
from jax.experimental.pallas import tpu as pltpu
from jax.sharding import PartitionSpec as P

LANES = 128
REACH = 7
SHIFTS = 16


def spline_taps(fraction):
    cube = fraction * fraction * fraction
    square = fraction * fraction
    first = (1.0 - fraction) ** 3 / 6.0
    second = (3.0 * cube - 6.0 * square + 4.0) / 6.0
    third = (-3.0 * cube + 3.0 * square + 3.0 * fraction + 1.0) / 6.0
    fourth = cube / 6.0
    return jnp.stack([first, second, third, fourth], axis=-1)


def kernel(
    lsts, chips, rows, blocks,
    coef_ref, vis_ref, flags_ref, level_ref, gains_ref, prior_ref, out_ref,
    ext, pair_out, pair_in, own, sum_out, sum_in,
    near_s, near_r, far_s, far_r, pair_s, pair_r, sum_s, sum_r, gat_s, gat_r, fwd_s, fwd_r,
):
    lst = lax.axis_index("lst")
    night = lax.axis_index("night")
    chip = night // 2
    core = night % 2
    partner = night + 1 - 2 * core
    groups = math.gcd(blocks, chips)
    splits = chips // groups
    phases = blocks // groups
    part = rows // splits
    piece = part // 2
    two_hops = lsts == 4
    if two_hops:
        odd = lst % 2
        near_to, near_at = lst + 1 - 2 * odd, 2 * odd * rows
        far_to, far_at = (lst + 2) % 4, 2 * odd * rows
        far_from = (2 - 2 * odd) * rows
    else:
        near_to, near_at = (lst + 1) % lsts, 0
        far_to, far_at = (lst + lsts - 1) % lsts, 2 * rows
        far_from = rows

    def remote(src, dst, send, recv, l, n):
        return pltpu.make_async_remote_copy(
            src_ref=src, dst_ref=dst, send_sem=send, recv_sem=recv,
            device_id={"lst": l, "night": n}, device_id_type=pl.DeviceIdType.MESH)

    others = [((chip + d) % chips) * 2 + core for d in range(1, chips)]
    barrier = pltpu.get_barrier_semaphore()
    greeted = [(near_to, night), (far_to, night), (lst, partner)] + [(lst, n) for n in others]
    for l, n in greeted:
        pl.semaphore_signal(barrier, inc=1, device_id={"lst": l, "night": n}, device_id_type=pl.DeviceIdType.MESH)

    def lanes(block):
        return pl.ds(pl.multiple_of(block * LANES, LANES), LANES)

    def near(t):
        return remote(ext.at[t, pl.ds(rows, rows)], ext.at[t, pl.ds(near_at, rows)],
                      near_s.at[t], near_r.at[t], near_to, night)

    def far(t):
        return remote(ext.at[t, pl.ds(far_from, rows)], ext.at[t, pl.ds(far_at, rows)],
                      far_s.at[t], far_r.at[t], far_to, night)

    def pass_on(t):
        near(t).wait_recv()
        if two_hops:
            far(t).start()

    def pair(s):
        return remote(pair_out.at[s], pair_in.at[s], pair_s.at[s], pair_r.at[s], lst, partner)

    def target(s):
        g, r = (s % chips) // splits, s % splits
        return (chip + 1 + g) % groups + ((chip // groups + 1 + r) % splits) * groups

    def toward(s):
        return remote(sum_out.at[s], sum_in.at[s], sum_s.at[s], sum_r.at[s], lst, target(s) * 2 + core)

    def place(owner, p, of_core):
        block = (owner % groups) * phases + p
        row = (owner // groups) * part + of_core * piece
        return out_ref.at[pl.ds(row, piece), :, :, lanes(block)]

    def gather(p, d):
        here = place(chip, p, core)
        i = p * chips + d
        return remote(here, here, gat_s.at[i], gat_r.at[i], lst, others[d - 1])

    def forward(p, d):
        here = place((chip + chips - d) % chips, p, core)
        i = p * chips + d
        return remote(here, here, fwd_s.at[i], fwd_r.at[i], lst, partner)

    def regrid(s, base, dst, index):
        t = s // splits

        def component(c, carry):
            acc = jnp.zeros((piece,) + ext.shape[3:], jnp.float32)
            for d in range(SHIFTS):
                window = ext[t, pl.ds(rows - REACH + d + base, piece), c]
                acc = acc + coef_ref[0, d] * window.astype(jnp.float32)
            dst[index, :, c] = acc.astype(dst.dtype)
            return carry

        lax.fori_loop(0, 3, component, 0)

    def first_part(s):
        base = ((chip // groups + 1 + s % splits) % splits) * part
        regrid(s, base + (1 - core) * piece, pair_out, s)
        pair(s).start()
        regrid(s, base + core * piece, own, s)

    def pair_sum(s):
        pair(s).wait_recv()
        both = own[s] + pair_in[s].astype(jnp.float32)
        if s % chips < chips - 1:
            sum_out[s] = both.astype(jnp.bfloat16)
            toward(s).start()
        else:
            own[s] = both

    def finish(p):
        total = own[p * chips + chips - 1]
        for k in range(chips - 1):
            toward(p * chips + k).wait_recv()
            total = total + sum_in[p * chips + k].astype(jnp.float32)
        block = (chip % groups) * phases + p
        prior = prior_ref[:, lanes(block)]
        den = total[:, 2]
        inverse = (den + prior[None])[:, None]
        row = (chip // groups) * part + core * piece
        out_ref[pl.ds(row, piece), 0:2, :, lanes(block)] = (total[:, 0:2] / inverse).astype(jnp.bfloat16)
        out_ref[pl.ds(row, piece), 2:3, :, lanes(block)] = den[:, None].astype(jnp.bfloat16)
        for d in range(1, chips):
            gather(p, d).start()
        forward(p, 0).start()

    def share(p):
        for d in range(1, chips):
            gather(p, d).wait_recv()
            forward(p, d).start()

    for t in range(blocks):
        block = ((chip + 1 + t % groups) % groups) * phases + t // groups
        scale = flags_ref[:, :, lanes(block)].astype(jnp.float32) * level_ref[:, :, lanes(block)]
        real_part = vis_ref[:, 0, :, lanes(block)].astype(jnp.float32)
        imag_part = vis_ref[:, 1, :, lanes(block)].astype(jnp.float32)
        gain_re = gains_ref[0:1, lanes(block)][None]
        gain_im = gains_ref[1:2, lanes(block)][None]
        cal_re = gain_re * real_part - gain_im * imag_part
        cal_im = gain_re * imag_part + gain_im * real_part
        ext[t, rows:2 * rows, 0] = (scale * cal_re).astype(jnp.bfloat16)
        ext[t, rows:2 * rows, 1] = (scale * cal_im).astype(jnp.bfloat16)
        ext[t, rows:2 * rows, 2] = scale.astype(jnp.bfloat16)
    pl.semaphore_wait(barrier, len(greeted))

    for t in range(blocks):
        near(t).start()
        if not two_hops:
            far(t).start()

    steps = phases * chips
    for t in range(min(1, blocks)):
        pass_on(t)
    for s in range(steps):
        t, p, k = s // splits, s // chips, s % chips
        if s % splits == 0:
            if t + 1 < blocks:
                pass_on(t + 1)
        if s > 0:
            pair_sum(s - 1)
        if p > 0 and k == 0:
            finish(p - 1)
        if p > 1 and k == chips - 1:
            share(p - 2)
        if s % splits == 0:
            far(t).wait_recv()
        first_part(s)
    pair_sum(steps - 1)
    finish(phases - 1)
    for p in range(max(phases - 2, 0), phases):
        share(p)
    for p in range(phases):
        for d in range(chips):
            forward(p, d).wait()
            if d > 0:
                gather(p, d).wait_send()
    for s in range(steps):
        pair(s).wait_send()
        if s % chips < chips - 1:
            toward(s).wait_send()
    for t in range(blocks):
        near(t).wait_send()
        far(t).wait_send()


def shards(mesh, visibility, flags, counts, offsets, fraction, gains, inverse_var, prior):
    lsts, chips = mesh.shape["lst"], mesh.shape["night"] // 2
    rows, baselines, channels = visibility.shape[1], visibility.shape[2], visibility.shape[4]
    blocks = channels // LANES
    level = (counts[0].astype(jnp.float32)[:, None] * inverse_var[0][None, :])[:, None, :]
    taps = spline_taps(fraction)[0].astype(jnp.bfloat16).astype(jnp.float32)
    shift = jnp.arange(SHIFTS).reshape(SHIFTS, 1)
    wanted = jnp.arange(4).reshape(1, 4) - offsets[0] - 1 + REACH
    coef = jnp.sum(jnp.where(shift == wanted, taps[None, :], 0.0), axis=1).reshape(1, SHIFTS)

    groups = math.gcd(blocks, chips)
    splits = chips // groups
    phases = blocks // groups
    steps = phases * chips
    piece = rows // splits // 2
    tile = (piece, 3, baselines, LANES)
    dma = pltpu.SemaphoreType.DMA
    out = pl.pallas_call(
        functools.partial(kernel, lsts, chips, rows, blocks),
        out_shape=jax.ShapeDtypeStruct((rows, 3, baselines, channels), jnp.bfloat16),
        in_specs=[
            pl.BlockSpec(memory_space=pltpu.SMEM),
        ] + [pl.BlockSpec(memory_space=pltpu.VMEM)] * 5,
        out_specs=pl.BlockSpec(memory_space=pltpu.VMEM),
        scratch_shapes=[
            pltpu.VMEM((blocks, 3 * rows, 3, baselines, LANES), jnp.bfloat16),
            pltpu.VMEM((steps,) + tile, jnp.bfloat16),
            pltpu.VMEM((steps,) + tile, jnp.bfloat16),
            pltpu.VMEM((steps,) + tile, jnp.float32),
            pltpu.VMEM((steps,) + tile, jnp.bfloat16),
            pltpu.VMEM((steps,) + tile, jnp.bfloat16),
            dma((blocks,)), dma((blocks,)), dma((blocks,)), dma((blocks,)),
            dma((steps,)), dma((steps,)), dma((steps,)), dma((steps,)),
            dma((steps,)), dma((steps,)), dma((steps,)), dma((steps,)),
        ],
        compiler_params=pltpu.CompilerParams(
            collective_id=0, has_side_effects=True, vmem_limit_bytes=40 * 2**20),
    )(coef, jnp.swapaxes(visibility[0], 1, 2), flags[0], level, gains[0], prior.reshape(1, channels))
    binned = jnp.swapaxes(out[:, 0:2], 1, 2)
    return binned, out[:, 2].astype(jnp.float32)


def solution(mesh):
    in_specs = (
        P("night", "lst", None, None, None),
        P("night", "lst", None, None),
        P("night", "lst"),
        P("night"),
        P("night"),
        P("night", None, None),
        P("night", None),
        P(),
    )
    out_specs = (P("lst", None, None, None), P("lst", None, None))
    return jax.shard_map(functools.partial(shards, mesh), mesh=mesh, in_specs=in_specs, out_specs=out_specs, check_vma=False)
```
